256 devices in a mesh: tile: 32 (over y, z_lo, core), freq: 8 (over z_hi, x).
Axes of the slice: x: 4, y: 4, z: 8 (z_hi: 2, z_lo: 4; z = z_hi * 4 + z_lo), core: 2. Of those that a mesh axis runs over, the one named last changes fastest.
Arguments:
- leaf_maps: bfloat16 [8, 65536, 2048], P('freq', 'tile'), as said below
- wave_index: int32 [8], P('freq'), may hold values from 0 to 7, as said below
- medium: bfloat16 [16384, 512], P('tile'), may hold values from 0.5 to 2
- source: bfloat16 [8, 16384, 512], P('freq', 'tile'), may hold values from -6 to 6
- state_field: bfloat16 [8, 16384, 512], P('freq', 'tile'), may hold values from -6 to 6
- adjoint_field: bfloat16 [8, 16384, 512], P('freq', 'tile'), may hold values from -6 to 6
- receivers: int32 [8, 8192], P('freq', 'tile'), may hold values from 0 to 262143
- recorded: bfloat16 [8, 8192], P('freq', 'tile'), may hold values from -180 to 180
Outputs:
- merged_maps: bfloat16 [8, 16384, 2048], P('freq', 'tile')
- medium_gradient: float32 [16384, 512], P(('tile', 'freq'))
The draws below stay inside these ranges and needn't reach their ends.
Inputs may be any that keep to these rules, and one draw needn't show every extreme that they name: leaf_maps: every leaf box map is exactly symmetric and positive definite. wave_index: the first eight frequencies (all of them if fewer) have distinct values.
All inputs are finite; a program needn't handle non-finite values.
Results may differ from the reference program's by a relative error of at most 0.0082.
Values may be sent and summed in bfloat16 or wider, within the bound.
No kernel may reach another device: no remote copies, remote signals or barrier semaphores. Data moves between devices by JAX's collectives and lax.ppermute only.
A program may use at most 192 MiB of HBM per device.

```python
import math
import jax
import jax.numpy as jnp
import numpy as np
from jax import lax

P_SIZE = 2048
BOX = 512
RECV = 256
FREQS = 8
LEAVES = 32
NX = 16384


def draw_wave_index(key, part):
    order = jax.random.permutation(jax.random.fold_in(key, 17), jnp.arange(8, dtype=jnp.int32))
    slots = jnp.arange(8, dtype=jnp.int32)
    place = jax.random.randint(jax.random.fold_in(key, 29), (), 0, min(FREQS, 8)).astype(jnp.int32)
    where_top = jnp.sum(jnp.where(order == 7, slots, 0)).astype(jnp.int32)
    moved = jnp.sum(jnp.where(slots == place, order, 0)).astype(jnp.int32)
    order = jnp.where(slots == place, 7, jnp.where(slots == where_top, moved, order)).astype(jnp.int32)
    return jnp.tile(order, FREQS // 8 + 1)[:FREQS].astype(jnp.int32)


def sign_rows(sub_key, rows):
    return (2 * jax.random.randint(sub_key, (rows, P_SIZE), 0, 2) - 1).astype(jnp.float32)


def draw_leaf_maps(key, part):
    quarter = P_SIZE // 4
    half_size = P_SIZE // 2
    column = jnp.arange(P_SIZE, dtype=jnp.float32)
    weights = 1.0 / (column + 1.0)
    weights = weights / jnp.mean(weights)
    root = jnp.sqrt(weights)
    common_key = jax.random.fold_in(key, 1000003)

    def one_map(index):
        quad = index // 4
        local = index % 4
        map_key = jax.random.fold_in(key, index)
        key_own, key_noise, key_shift, key_scales = jax.random.split(map_key, 4)
        quad_key = jax.random.fold_in(common_key, quad)
        level_two_key = jax.random.fold_in(quad_key, local % 2)
        level_one_key = jax.random.fold_in(quad_key, 2 + local // 2)
        divisor = 1.25 * P_SIZE
        shift = jnp.exp(jax.random.uniform(key_shift, (P_SIZE,), jnp.float32, math.log(0.15), math.log(0.4)))
        scales = jnp.exp(jax.random.uniform(key_scales, (P_SIZE,), jnp.float32, math.log(0.6), math.log(1.6)))
        base = jnp.concatenate([sign_rows(key_own, quarter), sign_rows(level_two_key, quarter), sign_rows(level_one_key, half_size)], axis=0)
        factor = (base + 0.5 * sign_rows(key_noise, P_SIZE)) * root[None, :]
        gram = jnp.dot(factor, factor.T, precision=lax.Precision.HIGHEST) / divisor
        gram = 0.5 * (gram + gram.T)
        outer = scales[:, None] * scales[None, :]
        identity = jnp.eye(P_SIZE, dtype=jnp.float32)
        full_map = gram * outer + shift[:, None] * identity
        return full_map.astype(jnp.bfloat16)
    maps = lax.map(one_map, jnp.arange(FREQS * LEAVES, dtype=jnp.int32))
    return maps.reshape(FREQS, LEAVES * P_SIZE, P_SIZE)


def draw_recorded(key, part):
    key_value, key_scale = jax.random.split(jax.random.fold_in(key, 4242))
    shape = (FREQS, LEAVES * RECV)
    value = jnp.clip(jax.random.normal(key_value, shape, jnp.float32), -6.0, 6.0)
    scale = jnp.exp(jax.random.uniform(key_scale, shape, jnp.float32, math.log(3.0), math.log(30.0)))
    return (value * scale).astype(jnp.bfloat16)


def plant(values, stream_key, low, top_value):
    spot = [jax.random.randint(jax.random.fold_in(stream_key, axis), (), 0, length) for axis, length in enumerate(values.shape)]
    longest = values.shape.index(max(values.shape))
    next_to = spot[:longest] + [(spot[longest] + 1) % values.shape[longest]] + spot[longest + 1:]
    return values.at[tuple(spot)].set(low).at[tuple(next_to)].set(top_value)


def shard_levels(key, shape, shards, low, largest):
    def one(position, parts):
        heights = jax.random.uniform(jax.random.fold_in(jax.random.fold_in(key, 6), position), (parts,), jnp.float32, low / len(shards), largest / len(shards))
        return jnp.repeat(jnp.exp(heights), shape[position] // parts).reshape((-1,) + (1,) * (len(shape) - position - 1))

    loudness = one(*shards[0])
    for cut in shards[1:]:
        loudness = loudness * one(*cut)
    return loudness


def bell_draw(key, shape, scale, most, cuts=(), kind=jnp.bfloat16):
    array = jax.random.normal(key, shape, jnp.float32) * scale
    if len(cuts) > 0:
        array = shard_levels(key, shape, cuts, -0.22, 0.18) * array
    return jnp.clip(array, min=-most, max=most).astype(kind)


def setup_inputs(seed: int = 0) -> dict:
    keys = jax.random.split(jax.random.key(seed), 9)
    leaf_maps = draw_leaf_maps(jax.random.fold_in(keys[8], 71), 0)
    wave_index = draw_wave_index(jax.random.fold_in(keys[8], 71), 0)
    medium = jnp.clip(jnp.exp(math.log(2.0) - 1.3862944 * jax.random.uniform(keys[2], (NX, BOX), jnp.float32) ** shard_levels(keys[2], (NX, BOX), ((0, 32),), -0.2, 0.2)), 0.5, 2.0).astype(jnp.bfloat16)
    source = bell_draw(keys[3], (FREQS, NX, BOX), 1.0, 6.0, ((0, 8), (1, 32)))
    state_field = bell_draw(keys[4], (FREQS, NX, BOX), 1.0, 6.0, ((0, 8), (1, 32)))
    adjoint_field = bell_draw(keys[5], (FREQS, NX, BOX), 1.0, 6.0, ((0, 8), (1, 32)))
    receivers = plant(jax.random.randint(keys[6], (FREQS, LEAVES * RECV), 0, BOX * BOX), jax.random.fold_in(keys[6], 1), 0, (BOX * BOX) - 1).astype(jnp.int32)
    recorded = draw_recorded(jax.random.fold_in(keys[8], 71), 0)
    return {"leaf_maps": leaf_maps, "wave_index": wave_index, "medium": medium, "source": source, "state_field": state_field, "adjoint_field": adjoint_field, "receivers": receivers, "recorded": recorded}


def merge_pair(left_map, right_map, exterior, interior):
    left_full = left_map.astype(jnp.float32)
    right_full = right_map.astype(jnp.float32)
    schur = left_full[interior][:, interior] + right_full[interior][:, interior]
    factor = jnp.linalg.cholesky(schur)
    solved_left = jax.scipy.linalg.solve_triangular(factor, left_full[exterior][:, interior].T, lower=True).astype(jnp.bfloat16)
    solved_right = jax.scipy.linalg.solve_triangular(factor, right_full[exterior][:, interior].T, lower=True).astype(jnp.bfloat16)
    columns = jnp.concatenate([solved_left, solved_right], axis=1).astype(jnp.float32)
    coupling = jnp.dot(columns.T, columns, precision=lax.Precision.HIGHEST)
    half_size = exterior.shape[0]
    zero_block = jnp.zeros((half_size, half_size), jnp.float32)
    upper = jnp.concatenate([left_full[exterior][:, exterior], zero_block], axis=1)
    lower = jnp.concatenate([zero_block, right_full[exterior][:, exterior]], axis=1)
    return (jnp.concatenate([upper, lower], axis=0) - coupling).astype(jnp.bfloat16)

def stencil(field):
    padded = jnp.pad(field, ((0, 0), (1, 1), (1, 1)))
    edges = padded[:, 2:, 1:-1] + padded[:, :-2, 1:-1] + padded[:, 1:-1, 2:] + padded[:, 1:-1, :-2]
    corners = padded[:, 2:, 2:] + padded[:, 2:, :-2] + padded[:, :-2, 2:] + padded[:, :-2, :-2]
    return (4.0 * edges + corners - 20.0 * field) / 6.0

def reference(leaf_maps, wave_index, medium, source, state_field, adjoint_field, receivers, recorded):
    half_size = P_SIZE // 2
    quarter = P_SIZE // 4
    outer_one = np.arange(0, half_size)
    inner_one = np.arange(half_size, P_SIZE)
    outer_two = np.concatenate([np.arange(0, quarter), np.arange(half_size, half_size + quarter)])
    inner_two = np.concatenate([np.arange(quarter, half_size), np.arange(half_size + quarter, P_SIZE)])

    def merge_quad(four_maps):
        first = merge_pair(four_maps[0], four_maps[1], outer_one, inner_one)
        second = merge_pair(four_maps[2], four_maps[3], outer_one, inner_one)
        return merge_pair(first, second, outer_two, inner_two)
    merged_list = []
    for freq_slot in range(FREQS):
        quads = leaf_maps[freq_slot].reshape(LEAVES // 4, 4, P_SIZE, P_SIZE)
        merged_list.append(lax.map(merge_quad, quads).reshape(LEAVES // 4 * P_SIZE, P_SIZE))
    merged_maps = jnp.stack(merged_list)
    kappa = 0.2 * (1.0 + wave_index.astype(jnp.float32))
    kappa_sq = (kappa * kappa)[:, None, None]
    medium_full = medium.astype(jnp.float32)[None]
    state_full = state_field.astype(jnp.float32)
    adjoint_full = adjoint_field.astype(jnp.float32)
    state_residual = source.astype(jnp.float32) - (stencil(state_full) + kappa_sq * medium_full * state_full)
    box_number = jnp.arange(LEAVES * RECV, dtype=jnp.int32) // RECV
    cells = (box_number[None, :] * BOX + receivers // BOX) * BOX + receivers % BOX
    flat_state = state_full.reshape(FREQS, NX * BOX)
    misfit = jnp.take_along_axis(flat_state, cells, axis=1) - recorded.astype(jnp.float32)
    freq_rows = jnp.broadcast_to(jnp.arange(FREQS, dtype=jnp.int32)[:, None], cells.shape)
    adjoint_source = jnp.zeros((FREQS, NX * BOX), jnp.float32).at[freq_rows, cells].add(misfit).reshape(FREQS, NX, BOX)
    adjoint_residual = adjoint_source - (stencil(adjoint_full) + kappa_sq * medium_full * adjoint_full)
    medium_gradient = -jnp.sum(kappa_sq * (state_full * state_residual + adjoint_full * adjoint_residual), axis=0)
    return (merged_maps, medium_gradient)
```

```python
import functools

import jax
import jax.numpy as jnp
from jax import lax
from jax.experimental import pallas as pl
from jax.experimental.pallas import tpu as pltpu
from jax.sharding import PartitionSpec as P

BLOCK = 128
SUB = 8
CHUNK = 256
VMEM_LIMIT = 56 * 1024 * 1024


def from_partner(block, axis, distance):
    count = lax.axis_size(axis)
    route = []
    for low in range(count):
        high = low | 1 << distance
        if high != low and high < count:
            route += [(low, high), (high, low)]
    return lax.ppermute(block, axis, route)


def extended(block, sides, width):
    for axis, dim in sides:
        count = lax.axis_size(axis)
        forward = [(i, i + 1) for i in range(count - 1)]
        backward = [(target, source) for source, target in forward]
        low = lax.ppermute(
            lax.slice_in_dim(block, block.shape[dim] - width, None, axis=dim), axis, forward
        )
        high = lax.ppermute(lax.slice_in_dim(block, 0, width, axis=dim), axis, backward)
        block = jnp.concatenate([low, block, high], axis=dim)
    return block


def ordered(flag, own_part, partner, axis_number):
    return jnp.where(
        flag == 0,
        jnp.concatenate([own_part, partner], axis=axis_number),
        jnp.concatenate([partner, own_part], axis=axis_number),
    )


def placed(flag, own_block, total_width):
    zero_block = jnp.zeros((own_block.shape[0], total_width - own_block.shape[1]), jnp.float32)
    return ordered(flag, own_block, zero_block, 1)


def split(x):
    high = x.astype(jnp.bfloat16)
    return high, (x - high.astype(jnp.float32)).astype(jnp.bfloat16)


def dot(a, b):
    return lax.dot_general(a, b, (((1,), (0,)), ((), ())), preferred_element_type=jnp.float32)


def lane_broadcast(x, lane):
    return jnp.broadcast_to(x[:, lane : lane + 1], x.shape)


def inverse_factor(rows):
    rows = list(rows)
    shape = rows[0].shape
    lane = lax.broadcasted_iota(jnp.int32, shape, 1)
    sub = lax.broadcasted_iota(jnp.int32, shape, 0)
    count = len(rows)
    for s in range(count):
        base = SUB * s
        pivots = (lane >= base) & (lane < base + SUB)
        spread = [jnp.broadcast_to(rows[s][a : a + 1, :], shape) for a in range(SUB)]
        entry = {
            (a, b): lane_broadcast(spread[a], base + b) for a in range(SUB) for b in range(a, SUB)
        }
        right = [
            jnp.where(pivots, jnp.where(lane == base + a, 1.0, 0.0), spread[a]) for a in range(SUB)
        ]
        left = {
            t: [lane_broadcast(rows[t], base + c) for c in range(SUB)] for t in range(s + 1, count)
        }
        scale, done, factor = [], [], {}
        if s + 1 < count:
            column = list(left[s + 1])
            following = jnp.where(pivots, 0.0, rows[s + 1])
        for j in range(SUB):
            r = lax.rsqrt(entry[j, j])
            scale.append(r)
            for b in range(j + 1, SUB):
                factor[b, j] = entry[j, b] * r
            for a in range(j + 1, SUB):
                for b in range(a, SUB):
                    entry[a, b] = entry[a, b] - factor[a, j] * factor[b, j]
            row = right[j] * r
            done.append(row)
            for a in range(j + 1, SUB):
                right[a] = right[a] - factor[a, j] * row
            if s + 1 < count:
                weight = column[j] * r
                for a in range(j + 1, SUB):
                    column[a] = column[a] - weight * factor[a, j]
                following = following - weight * row
        group = done[SUB - 1]
        for a in range(SUB - 1):
            group = jnp.where(sub == a, done[a], group)
        rows[s] = group
        if s + 1 < count:
            rows[s + 1] = following
        if s + 2 < count:
            solved = list(done)
            for c in range(SUB - 1, -1, -1):
                solved[c] = solved[c] * scale[c]
                for a in range(c):
                    solved[a] = solved[a] - factor[c, a] * solved[c]
            for t in range(s + 2, count):
                value = jnp.where(pivots, 0.0, rows[t])
                for c in range(SUB):
                    value = value - left[t][c] * solved[c]
                rows[t] = value
    return [jnp.where(lane <= sub + SUB * s, rows[s], 0.0) for s in range(count)]


def column_chunks(start, stop):
    chunks = []
    while start < stop:
        end = min(stop, (start // CHUNK + 1) * CHUNK)
        chunks.append((start, end))
        start = end
    return chunks


def solve_kernel(own_ref, other_ref, right_ref, out_ref, work_ref, panel_ref, left_ref):
    size, width = right_ref.shape
    blocks = size // BLOCK
    total = size + width
    for i in range(blocks):
        r = slice(i * BLOCK, (i + 1) * BLOCK)
        work_ref[r, i * BLOCK : size] = own_ref[r, i * BLOCK :].astype(jnp.float32) + other_ref[
            r, i * BLOCK :
        ].astype(jnp.float32)
        work_ref[r, size:] = right_ref[r, :].astype(jnp.float32)
    for k in range(blocks):
        start = k * BLOCK
        stop = start + BLOCK
        r = slice(start, stop)
        rows = [
            work_ref[start + SUB * s : start + SUB * (s + 1), start:stop]
            for s in range(BLOCK // SUB)
        ]
        high, low = split(jnp.concatenate(inverse_factor(rows), axis=0))
        both = jnp.concatenate([high, low], axis=1)
        for c0, c1 in column_chunks(stop, total):
            work_high, work_low = split(work_ref[r, c0:c1])
            panel = dot(both, jnp.concatenate([work_high, work_high], axis=0)) + dot(high, work_low)
            panel_high, panel_low = split(panel)
            panel_ref[:BLOCK, c0:c1] = panel_high
            panel_ref[BLOCK:, c0:c1] = panel_low
            if c0 >= size:
                out_ref[c0 - size : c1 - size, r] = panel_high.T
            else:
                for c in range(c0, c1, BLOCK):
                    turned_high, turned_low = split(panel[:, c - c0 : c - c0 + BLOCK].T)
                    left_ref[c : c + BLOCK, :BLOCK] = turned_high
                    left_ref[c : c + BLOCK, BLOCK:] = turned_low
        for i0, i1 in ((k + 1, k + 2), (k + 2, blocks)):
            if i0 >= blocks:
                continue
            for c0, c1 in column_chunks(i0 * BLOCK, total):
                q = slice(i0 * BLOCK, min(i1 * BLOCK, c1))
                panel_high = panel_ref[:BLOCK, c0:c1]
                update = dot(
                    left_ref[q, :], jnp.concatenate([panel_high, panel_high], axis=0)
                ) + dot(left_ref[q, :BLOCK], panel_ref[BLOCK:, c0:c1])
                work_ref[q, c0:c1] = work_ref[q, c0:c1] - update


def solved_columns(own, other, right, own_spec, right_spec, width):
    size = other.shape[0]
    return pl.pallas_call(
        solve_kernel,
        grid=(1,),
        out_shape=jax.ShapeDtypeStruct((width, size), jnp.bfloat16),
        in_specs=[own_spec, pl.BlockSpec((size, size), lambda g: (0, 0)), right_spec],
        out_specs=pl.BlockSpec((width, size), lambda g: (0, 0)),
        scratch_shapes=[
            pltpu.VMEM((size, size + width), jnp.float32),
            pltpu.VMEM((2 * BLOCK, size + width), jnp.bfloat16),
            pltpu.VMEM((size, 2 * BLOCK), jnp.bfloat16),
        ],
        compiler_params=pltpu.CompilerParams(vmem_limit_bytes=VMEM_LIMIT),
        cost_estimate=pl.CostEstimate(
            flops=60_000_000_000, bytes_accessed=8_000_000, transcendentals=0
        ),
    )(own, other, right)


def product(a, b):
    return lax.dot_general(a, b, (((1,), (1,)), ((), ())), preferred_element_type=jnp.float32)


def maps_merged(leaf_map, low_bit, high_bit, partner_inner):
    half = leaf_map.shape[0] // 2
    quarter = half // 2
    solved_own = solved_columns(
        leaf_map,
        partner_inner,
        leaf_map,
        pl.BlockSpec((half, half), lambda g: (1, 1)),
        pl.BlockSpec((half, half), lambda g: (1, 0)),
        half,
    )
    solved_partner = from_partner(solved_own, "tile", 0)
    own_outer, own_inner = solved_own[:quarter], solved_own[quarter:]
    partner_outer, partner_inner = solved_partner[:quarter], solved_partner[quarter:]
    inner_all = ordered(low_bit, own_inner, partner_inner, 0)
    outer_all = ordered(low_bit, own_outer, partner_outer, 0)
    block = leaf_map[:half, :half].astype(jnp.float32)
    inner_rows = (
        placed(low_bit, block[quarter:, quarter:], half) - product(own_inner, inner_all)
    ).astype(jnp.bfloat16)
    sibling_rows = from_partner(inner_rows, "tile", 1)
    sum_rows = inner_rows.astype(jnp.float32) + sibling_rows.astype(jnp.float32)
    outer_rows = (
        placed(low_bit, block[:quarter, :quarter], half) - product(own_outer, outer_all)
    ).astype(jnp.bfloat16)
    zero = jnp.zeros((quarter, quarter), jnp.float32)
    right = (
        ordered(low_bit, block[quarter:, :quarter], zero, 0) - product(inner_all, own_outer)
    ).astype(jnp.bfloat16)
    partner_sum = from_partner(sum_rows, "tile", 0)
    schur = ordered(low_bit, sum_rows, partner_sum, 0)
    solved_own = solved_columns(
        schur,
        jnp.zeros((half, half), jnp.bfloat16),
        right,
        pl.BlockSpec((half, half), lambda g: (0, 0)),
        pl.BlockSpec((half, quarter), lambda g: (0, 0)),
        quarter,
    )
    solved_partner = from_partner(solved_own, "tile", 0)
    solved_pair = ordered(low_bit, solved_own, solved_partner, 0)
    solved_sibling = from_partner(solved_pair, "tile", 1)
    solved_all = ordered(high_bit, solved_pair, solved_sibling, 0)
    own_block = outer_rows.astype(jnp.float32)
    return (placed(high_bit, own_block, 2 * half) - product(solved_own, solved_all)).astype(
        jnp.bfloat16
    )


def stencil(padded, field):
    edges = (
        padded[..., 2:, 1:-1]
        + padded[..., :-2, 1:-1]
        + padded[..., 1:-1, 2:]
        + padded[..., 1:-1, :-2]
    )
    corners = (
        padded[..., 2:, 2:] + padded[..., 2:, :-2] + padded[..., :-2, 2:] + padded[..., :-2, :-2]
    )
    return (4.0 * edges + corners - 20.0 * field) / 6.0


def gradient(wave_index, medium, source, state_field, adjoint_field, receivers, recorded):
    stacked = jnp.stack([state_field, adjoint_field])
    rimmed = extended(stacked, (("tile", 2),), 1)
    rimmed = jnp.pad(rimmed.astype(jnp.float32), ((0, 0), (0, 0), (0, 0), (1, 1)))
    fields = stacked.astype(jnp.float32)
    kappa = 0.2 * (1.0 + wave_index.astype(jnp.float32))
    kappa_sq = (kappa * kappa)[:, None, None]
    medium_full = medium.astype(jnp.float32)[None]
    applied = stencil(rimmed, fields) + kappa_sq[None] * medium_full[None] * fields
    state_full = fields[0]
    adjoint_full = fields[1]
    state_residual = source.astype(jnp.float32) - applied[0]
    box_cells = state_full.shape[1] * state_full.shape[2]
    flat_state = state_full.reshape(state_full.shape[0], box_cells)
    misfit = jnp.take_along_axis(flat_state, receivers, axis=1) - recorded.astype(jnp.float32)
    freq_rows = jnp.broadcast_to(
        jnp.arange(receivers.shape[0], dtype=jnp.int32)[:, None], receivers.shape
    )
    adjoint_source = (
        jnp.zeros(flat_state.shape, jnp.float32)
        .at[freq_rows, receivers]
        .add(misfit)
        .reshape(state_full.shape)
    )
    adjoint_residual = adjoint_source - applied[1]
    gradient_term = -jnp.sum(
        kappa_sq * (state_full * state_residual + adjoint_full * adjoint_residual), axis=0
    )
    return gradient_term


def body(leaf_maps, wave_index, medium, source, state_field, adjoint_field, receivers, recorded):
    tile_index = lax.axis_index("tile")
    low_bit = jnp.bitwise_and(tile_index, 1)
    high_bit = jnp.bitwise_and(jnp.right_shift(tile_index, 1), 1)
    leaf_map = leaf_maps[0]
    half = leaf_map.shape[0] // 2
    partner_inner = from_partner(leaf_map[half:, half:], "tile", 0)
    gradient_term = gradient(
        wave_index, medium, source, state_field, adjoint_field, receivers, recorded
    )
    partner_inner, gradient_term = lax.optimization_barrier((partner_inner, gradient_term))
    medium_gradient = lax.psum_scatter(gradient_term, "freq", scatter_dimension=0, tiled=True)
    merged_maps = maps_merged(leaf_map, low_bit, high_bit, partner_inner)[None]
    return (merged_maps, medium_gradient)


def solution(mesh):
    placed = (
        P("freq", "tile", None),
        P("freq"),
        P("tile", None),
        P("freq", "tile", None),
        P("freq", "tile", None),
        P("freq", "tile", None),
        P("freq", "tile"),
        P("freq", "tile"),
    )
    return jax.shard_map(
        body,
        mesh=mesh,
        in_specs=placed,
        out_specs=(P("freq", "tile", None), P(("tile", "freq"), None)),
        check_vma=False,
    )
```

```python
import functools

import jax
import jax.numpy as jnp
from jax import lax
from jax.experimental import pallas as pl
from jax.experimental.pallas import tpu as pltpu
from jax.sharding import PartitionSpec as P

BLOCK = 128
SUB = 8
CHUNK = 256
PANEL = 8
AHEAD = 3
MIB = 1024 * 1024


def from_partner(block, axis, distance):
    count = lax.axis_size(axis)
    route = []
    for low in range(count):
        high = low | 1 << distance
        if high != low and high < count:
            route += [(low, high), (high, low)]
    return lax.ppermute(block, axis, route)


def split(x):
    high = x.astype(jnp.bfloat16)
    return high, (x - high.astype(jnp.float32)).astype(jnp.bfloat16)


def dot(a, b):
    return lax.dot_general(a, b, (((1,), (0,)), ((), ())), preferred_element_type=jnp.float32)


def lane_broadcast(x, lane):
    return jnp.broadcast_to(x[:, lane : lane + 1], x.shape)


def sublane_broadcast(ref, row, shape):
    return jnp.broadcast_to(ref[row : row + 1, :], shape)


def inverse_factor(rows, scratch):
    group_ref, entry_ref, weight_ref = scratch
    rows = list(rows)
    shape = rows[0].shape
    lane = lax.broadcasted_iota(jnp.int32, shape, 1)
    sub = lax.broadcasted_iota(jnp.int32, shape, 0)
    count = len(rows)
    current = [lane_broadcast(rows[0], c) for c in range(SUB)]
    weights = [lane_broadcast(rows[1], c) for c in range(SUB)]
    for s in range(count):
        base = SUB * s
        panel = s // PANEL * PANEL
        reach = min(count, panel + PANEL + AHEAD)
        pivots = (lane >= base) & (lane < base + SUB)
        slot = s % 2 * SUB
        bank = slot * SUB
        group_ref[slot : slot + SUB, :] = rows[s]
        for c in range(SUB):
            entry_ref[bank + SUB * c : bank + SUB * (c + 1), :] = current[c]
        entry = {
            (a, b): sublane_broadcast(entry_ref, bank + SUB * b + a, shape)
            for a in range(SUB)
            for b in range(a, SUB)
        }
        right = [
            jnp.where(
                pivots,
                jnp.where(lane == base + a, 1.0, 0.0),
                sublane_broadcast(group_ref, slot + a, shape),
            )
            for a in range(SUB)
        ]
        left = {
            t: [lane_broadcast(rows[t], base + c) for c in range(SUB)] for t in range(s + 2, reach)
        }
        one, two = s + 1 < count, s + 2 < count
        if one:
            column = list(weights)
            following = jnp.where(pivots, 0.0, rows[s + 1])
            current = [lane_broadcast(rows[s + 1], base + SUB + c) for c in range(SUB)]
        if two:
            second = list(left[s + 2])
            later = jnp.where(pivots, 0.0, rows[s + 2])
            weights = [lane_broadcast(rows[s + 2], base + SUB + c) for c in range(SUB)]
        scale, done, factor = [], [], {}
        for j in range(SUB):
            r = lax.rsqrt(entry[j, j])
            scale.append(r)
            for b in range(j + 1, SUB):
                factor[b, j] = entry[j, b] * r
            for a in range(j + 1, SUB):
                for b in range(a, SUB):
                    entry[a, b] = entry[a, b] - factor[a, j] * factor[b, j]
            row = right[j] * r
            done.append(row)
            for a in range(j + 1, SUB):
                right[a] = right[a] - factor[a, j] * row
            if one:
                weight = column[j] * r
                for a in range(j + 1, SUB):
                    column[a] = column[a] - weight * factor[a, j]
                following = following - weight * row
                place = bank + SUB * j
                weight_ref[place : place + SUB, :] = weight
                spread = [sublane_broadcast(weight_ref, place + c, shape) for c in range(SUB)]
                current = [current[c] - weight * spread[c] for c in range(SUB)]
            if two:
                weight = second[j] * r
                for a in range(j + 1, SUB):
                    second[a] = second[a] - weight * factor[a, j]
                later = later - weight * row
                weights = [weights[c] - weight * spread[c] for c in range(SUB)]
        group = done[SUB - 1]
        for a in range(SUB - 1):
            group = jnp.where(sub == a, done[a], group)
        rows[s] = group
        if one:
            rows[s + 1] = following
        if two:
            rows[s + 2] = later
        if s + 3 < reach:
            solved = list(done)
            for c in range(SUB - 1, -1, -1):
                solved[c] = solved[c] * scale[c]
                for a in range(c):
                    solved[a] = solved[a] - factor[c, a] * solved[c]
            for t in range(s + 3, reach):
                value = jnp.where(pivots, 0.0, rows[t])
                for c in range(SUB):
                    value = value - left[t][c] * solved[c]
                rows[t] = value
        if s == panel + PANEL - 1 and reach < count:
            block = jnp.concatenate(rows[panel : s + 1], axis=0)
            low, high = SUB * panel, SUB * (panel + PANEL)
            block_lane = lax.broadcasted_iota(jnp.int32, block.shape, 1)
            block_row = lax.broadcasted_iota(jnp.int32, block.shape, 0) + low
            right_high, right_low = split(
                jnp.where((block_lane < high) & (block_lane > block_row), 0.0, block)
            )
            left_high, left_low = split(block.T[SUB * reach :, :])
            update = dot(
                jnp.concatenate([left_high, left_high, left_low], axis=1),
                jnp.concatenate([right_high, right_low, right_high], axis=0),
            )
            inside = (lane >= low) & (lane < high)
            for t in range(reach, count):
                q = slice(SUB * (t - reach), SUB * (t - reach + 1))
                rows[t] = jnp.where(inside, 0.0, rows[t]) - update[q, :]
    return [jnp.where(lane <= sub + SUB * s, rows[s], 0.0) for s in range(count)]


def inverse_scratch():
    return [
        pltpu.VMEM((2 * SUB, BLOCK), jnp.float32),
        pltpu.VMEM((2 * SUB * SUB, BLOCK), jnp.float32),
        pltpu.VMEM((2 * SUB * SUB, BLOCK), jnp.float32),
    ]


def column_chunks(start, stop):
    chunks = []
    while start < stop:
        end = min(stop, (start // CHUNK + 1) * CHUNK)
        chunks.append((start, end))
        start = end
    return chunks


def split_three(x):
    high = x.astype(jnp.bfloat16)
    rest = x - high.astype(jnp.float32)
    middle = rest.astype(jnp.bfloat16)
    return high, middle, (rest - middle.astype(jnp.float32)).astype(jnp.bfloat16)


def dot_turned(a, b):
    return lax.dot_general(a, b, (((1,), (1,)), ((), ())), preferred_element_type=jnp.float32)


def in_vmem(count):
    return [pl.BlockSpec(memory_space=pltpu.VMEM)] * count


def in_any(count):
    return [pl.BlockSpec(memory_space=pl.ANY)] * count


def estimate(us):
    return pl.CostEstimate(
        flops=int(us * 800_000_000), bytes_accessed=int(us * 1_000_000), transcendentals=0
    )


def params(mib):
    return pltpu.CompilerParams(vmem_limit_bytes=mib * MIB)


def factor_and_solve(entries, rights, ready, refs, size, width, out_ref, keep):
    work_ref, panel_ref, left_ref = refs[:3]
    scratch = refs[3:]
    blocks = size // BLOCK
    total = size + width

    def start_value(i0, i1, c0, c1):
        source = entries if c0 < size else rights
        shift = 0 if c0 < size else size
        return jnp.concatenate([source(i, c0 - shift, c1 - shift) for i in range(i0, i1)], axis=0)

    for k in range(blocks):
        start = k * BLOCK
        stop = start + BLOCK
        r = slice(start, stop)
        if k == 0:
            block = entries(0, 0, BLOCK)
        else:
            block = work_ref[r, start:stop]
        rows = [block[SUB * s : SUB * (s + 1), :] for s in range(BLOCK // SUB)]
        high, low = split(jnp.concatenate(inverse_factor(rows, scratch), axis=0))
        both = jnp.concatenate([high, low], axis=1)
        if k == 0:
            ready()
        if keep is not None:
            keep[0][r, :] = both
        for c0, c1 in column_chunks(stop, total):
            value = start_value(0, 1, c0, c1) if k == 0 else work_ref[r, c0:c1]
            work_high, work_low = split(value)
            panel = dot(both, jnp.concatenate([work_high, work_high], axis=0)) + dot(high, work_low)
            panel_high, panel_low = split(panel)
            panel_ref[:BLOCK, c0:c1] = panel_high
            panel_ref[BLOCK:, c0:c1] = panel_low
            if c0 >= size:
                out_ref[c0 - size : c1 - size, r] = panel_high.T
            else:
                for c in range(c0, c1, BLOCK):
                    turned_high, turned_low = split(panel[:, c - c0 : c - c0 + BLOCK].T)
                    left_ref[c : c + BLOCK, :BLOCK] = turned_high
                    left_ref[c : c + BLOCK, BLOCK:] = turned_low
                    if keep is not None:
                        q = slice(c - BLOCK, c)
                        keep[1][q, 2 * start : 2 * start + BLOCK] = turned_high
                        keep[1][q, 2 * start + BLOCK : 2 * stop] = turned_low
        for i0, i1 in ((k + 1, k + 2), (k + 2, blocks)):
            if i0 >= blocks:
                continue
            for c0, c1 in column_chunks(i0 * BLOCK, total):
                i2 = min(i1, c1 // BLOCK)
                q = slice(i0 * BLOCK, i2 * BLOCK)
                panel_high = panel_ref[:BLOCK, c0:c1]
                update = dot(
                    left_ref[q, :], jnp.concatenate([panel_high, panel_high], axis=0)
                ) + dot(left_ref[q, :BLOCK], panel_ref[BLOCK:, c0:c1])
                value = start_value(i0, i2, c0, c1) if k == 0 else work_ref[q, c0:c1]
                work_ref[q, c0:c1] = value - update


def elimination_scratch(size, width):
    return [
        pltpu.VMEM((size, size + width), jnp.float32),
        pltpu.VMEM((2 * BLOCK, size + width), jnp.bfloat16),
        pltpu.VMEM((size, 2 * BLOCK), jnp.bfloat16),
        *inverse_scratch(),
    ]


def packed_offsets(size):
    offsets, lane = [], 0
    for b in range(size // BLOCK):
        offsets.append(lane)
        lane += size - b * BLOCK
    return offsets, lane


def first_kernel(leaf_ref, other_ref, out_ref, triangle_ref, *scratch):
    own_v, other_v, right_v, inner_v = scratch[:4]
    elimination, sems = scratch[4:-1], scratch[-1]
    size = other_v.shape[0]
    width = right_v.shape[1]
    quarter = inner_v.shape[0]
    first = slice(0, BLOCK)
    rest = slice(BLOCK, size)

    def copies(rows, position):
        lower = slice(size + rows.start, size + rows.stop)
        return [
            pltpu.make_async_copy(
                leaf_ref.at[0, lower, pl.ds(size, size)], own_v.at[rows, :], sems.at[position]
            ),
            pltpu.make_async_copy(
                other_ref.at[rows, :], other_v.at[rows, :], sems.at[position + 1]
            ),
            pltpu.make_async_copy(
                leaf_ref.at[0, lower, pl.ds(0, width)], right_v.at[rows, :], sems.at[position + 2]
            ),
        ]

    early, late = copies(first, 0), copies(rest, 3)
    inner = pltpu.make_async_copy(
        leaf_ref.at[0, pl.ds(quarter, quarter), pl.ds(quarter, quarter)], inner_v, sems.at[6]
    )
    for copy in early + late + [inner]:
        copy.start()
    early[0].wait()
    early[1].wait()

    def entries(i, c0, c1):
        r = slice(i * BLOCK, (i + 1) * BLOCK)
        return own_v[r, c0:c1].astype(jnp.float32) + other_v[r, c0:c1].astype(jnp.float32)

    def rights(i, c0, c1):
        return right_v[i * BLOCK : (i + 1) * BLOCK, c0:c1].astype(jnp.float32)

    def ready():
        for copy in [early[2]] + late + [inner]:
            copy.wait()

    factor_and_solve(entries, rights, ready, elimination, size, width, out_ref, None)
    offsets, _ = packed_offsets(quarter)
    for b in range(quarter // BLOCK):
        r = slice(b * BLOCK, (b + 1) * BLOCK)
        c = slice(b * BLOCK, quarter)
        value = inner_v[r, c].astype(jnp.float32) - dot_turned(
            out_ref[quarter + r.start : quarter + r.stop, :],
            out_ref[quarter + c.start : quarter + c.stop, :],
        )
        triangle_ref[:, offsets[b] : offsets[b] + quarter - b * BLOCK] = value.astype(jnp.bfloat16)


def first_solve(leaf_maps, partner_inner):
    size = partner_inner.shape[0]
    width = leaf_maps.shape[2] - size
    quarter = width // 2
    _, lanes = packed_offsets(quarter)
    return pl.pallas_call(
        first_kernel,
        out_shape=(
            jax.ShapeDtypeStruct((width, size), jnp.bfloat16),
            jax.ShapeDtypeStruct((BLOCK, lanes), jnp.bfloat16),
        ),
        in_specs=in_any(2),
        out_specs=tuple(in_vmem(2)),
        scratch_shapes=[
            pltpu.VMEM((size, size), jnp.bfloat16),
            pltpu.VMEM((size, size), jnp.bfloat16),
            pltpu.VMEM((size, width), jnp.bfloat16),
            pltpu.VMEM((quarter, quarter), jnp.bfloat16),
            *elimination_scratch(size, width),
            pltpu.SemaphoreType.DMA((7,)),
        ],
        compiler_params=params(57),
        cost_estimate=estimate(30),
        name="level_one_solve",
    )(leaf_maps, partner_inner)


def cross_interface_kernel(low_ref, solved_ref, partner_ref, out_ref, part_ref):
    low = low_ref[0]
    half = part_ref.shape[0]

    @pl.when(low == 0)
    def _():
        out_ref[...] = (-dot_turned(solved_ref[...], partner_ref[...])).astype(jnp.bfloat16)

    @pl.when(low != 0)
    def _():
        out_ref[...] = (-dot_turned(partner_ref[...], solved_ref[...])).astype(jnp.bfloat16)

    part_ref[...] = out_ref[pl.ds(pl.multiple_of(low * half, half), half), :]


def cross_interface(low, solved, partner):
    quarter = solved.shape[0] // 2
    inner = pl.BlockSpec((quarter, solved.shape[1]), lambda g: (1, 0))
    return pl.pallas_call(
        cross_interface_kernel,
        grid=(1,),
        out_shape=(
            jax.ShapeDtypeStruct((quarter, quarter), jnp.bfloat16),
            jax.ShapeDtypeStruct((quarter // 2, quarter), jnp.bfloat16),
        ),
        in_specs=[pl.BlockSpec(memory_space=pltpu.SMEM), inner, inner],
        out_specs=(
            pl.BlockSpec((quarter, quarter), lambda g: (0, 0)),
            pl.BlockSpec((quarter // 2, quarter), lambda g: (0, 0)),
        ),
        compiler_params=params(16),
        cost_estimate=estimate(2),
        name="cross_interface",
    )(low, solved, partner)


def outer_kernel(low_ref, leaf_ref, solved_ref, partner_ref, outer_ref, right_ref):
    quarter = outer_ref.shape[0]
    low = low_ref[0]
    here = pl.ds(pl.multiple_of(low * quarter, quarter), quarter)
    there = pl.ds(pl.multiple_of((1 - low) * quarter, quarter), quarter)
    own = solved_ref[:quarter, :]
    outer_ref[:, here] = (
        leaf_ref[0, :quarter, :].astype(jnp.float32) - dot_turned(own, own)
    ).astype(jnp.bfloat16)
    right_ref[here, :] = (
        leaf_ref[0, quarter:, :].astype(jnp.float32) - dot_turned(solved_ref[quarter:, :], own)
    ).astype(jnp.bfloat16)
    outer_ref[:, there] = (-dot_turned(own, partner_ref[:quarter, :])).astype(jnp.bfloat16)
    right_ref[there, :] = (-dot_turned(partner_ref[quarter:, :], own)).astype(jnp.bfloat16)


def outer_blocks(low, columns, solved, partner):
    half = solved.shape[0]
    quarter = half // 2
    whole = pl.BlockSpec(solved.shape, lambda g: (0, 0))
    return pl.pallas_call(
        outer_kernel,
        grid=(1,),
        out_shape=(
            jax.ShapeDtypeStruct((quarter, half), jnp.bfloat16),
            jax.ShapeDtypeStruct((half, quarter), jnp.bfloat16),
        ),
        in_specs=[
            pl.BlockSpec(memory_space=pltpu.SMEM),
            pl.BlockSpec((1, half, quarter), lambda g: (0, 0, 0)),
            whole,
            whole,
        ],
        out_specs=(
            pl.BlockSpec((quarter, half), lambda g: (0, 0)),
            pl.BlockSpec((half, quarter), lambda g: (0, 0)),
        ),
        compiler_params=params(16),
        cost_estimate=estimate(5),
        name="outer_blocks",
    )(low, columns, solved, partner)


def second_kernel(low_ref, *refs):
    (own_t, partner_t, sibling_t, far_t, cross_h, sibling_c, far_c, right_h) = refs[:8]
    out_ref, inverse_ref, lower_ref = refs[8:11]
    here_v, there_v, cross_v, other_v, right_v = refs[11:16]
    elimination, sems = refs[16:-1], refs[-1]
    low = low_ref[0]
    quarter = cross_v.shape[0]
    size = 2 * quarter
    width = right_v.shape[1]
    half = quarter // 2
    offsets, _ = packed_offsets(quarter)
    moves = [
        (own_t, here_v.at[low]),
        (partner_t, here_v.at[1 - low]),
        (sibling_t, there_v.at[low]),
        (far_t, there_v.at[1 - low]),
        (cross_h, cross_v),
        (sibling_c, other_v.at[low]),
        (far_c, other_v.at[1 - low]),
        (right_h, right_v),
    ]
    copies = [
        pltpu.make_async_copy(source, target, sems.at[n]) for n, (source, target) in enumerate(moves)
    ]
    for copy in copies:
        copy.start()
    for copy in copies[:4]:
        copy.wait()

    def entries(i, c0, c1):
        parts = []
        b = i % (quarter // BLOCK)
        side = i // (quarter // BLOCK)
        inner_end = quarter * (side + 1)
        if c0 < inner_end:
            lanes = slice(offsets[b] + c0 - i * BLOCK, offsets[b] + min(c1, inner_end) - i * BLOCK)
            parts.append(
                here_v[side, :, lanes].astype(jnp.float32)
                + there_v[side, :, lanes].astype(jnp.float32)
            )
        if c1 > inner_end:
            lanes = slice(max(c0, inner_end) - quarter, c1 - quarter)
            top = (i * BLOCK) % half
            parts.append(
                cross_v[i * BLOCK : (i + 1) * BLOCK, lanes].astype(jnp.float32)
                + other_v[i * BLOCK // half, top : top + BLOCK, lanes].astype(jnp.float32)
            )
        return parts[0] if len(parts) == 1 else jnp.concatenate(parts, axis=1)

    def rights(i, c0, c1):
        return right_v[i * BLOCK : (i + 1) * BLOCK, c0:c1].astype(jnp.float32)

    def ready():
        for copy in copies[4:]:
            copy.wait()

    factor_and_solve(
        entries,
        rights,
        ready,
        elimination,
        size,
        width,
        out_ref,
        (inverse_ref, lower_ref),
    )


def second_solve(low, triangles, cross, cross_parts, right):
    size, width = right.shape
    quarter = size // 2
    lanes = triangles[0].shape[1]
    return pl.pallas_call(
        second_kernel,
        out_shape=(
            jax.ShapeDtypeStruct((width, size), jnp.bfloat16),
            jax.ShapeDtypeStruct((size, 2 * BLOCK), jnp.bfloat16),
            jax.ShapeDtypeStruct((size - BLOCK, 2 * (size - BLOCK)), jnp.bfloat16),
        ),
        in_specs=[pl.BlockSpec(memory_space=pltpu.SMEM), *in_any(8)],
        out_specs=tuple(in_vmem(3)),
        scratch_shapes=[
            pltpu.VMEM((2, BLOCK, lanes), jnp.bfloat16),
            pltpu.VMEM((2, BLOCK, lanes), jnp.bfloat16),
            pltpu.VMEM((quarter, quarter), jnp.bfloat16),
            pltpu.VMEM((2, quarter // 2, quarter), jnp.bfloat16),
            pltpu.VMEM((size, width), jnp.bfloat16),
            *elimination_scratch(size, width),
            pltpu.SemaphoreType.DMA((8,)),
        ],
        compiler_params=params(32),
        cost_estimate=estimate(30),
        name="level_two_solve",
    )(low, *triangles, cross, *cross_parts, right)


def substitution_kernel(inverse_ref, lower_ref, right_ref, out_ref, work_ref):
    size, width = right_ref.shape
    blocks = size // BLOCK
    for k in range(blocks):
        r = slice(k * BLOCK, (k + 1) * BLOCK)
        both = inverse_ref[r, :]
        left = lower_ref[k * BLOCK :, 2 * k * BLOCK : 2 * (k + 1) * BLOCK] if k + 1 < blocks else None
        for c0, c1 in column_chunks(0, width):
            c = slice(c0, c1)
            value = right_ref[r, c].astype(jnp.float32) if k == 0 else work_ref[r, c]
            high, low = split(value)
            panel = dot(both, jnp.concatenate([high, high], axis=0)) + dot(both[:, :BLOCK], low)
            high, low = split(panel)
            out_ref[c, r] = high.T
            if left is None:
                continue
            q = slice((k + 1) * BLOCK, size)
            update = dot(left, jnp.concatenate([high, high], axis=0)) + dot(left[:, :BLOCK], low)
            value = right_ref[q, c].astype(jnp.float32) if k == 0 else work_ref[q, c]
            work_ref[q, c] = value - update


def substitution(inverse, lower, right):
    size, width = right.shape
    return pl.pallas_call(
        substitution_kernel,
        out_shape=jax.ShapeDtypeStruct((width, size), jnp.bfloat16),
        in_specs=in_vmem(3),
        out_specs=pl.BlockSpec(memory_space=pltpu.VMEM),
        scratch_shapes=[pltpu.VMEM((size, width), jnp.float32)],
        compiler_params=params(16),
        cost_estimate=estimate(6),
        name="sibling_solve",
    )(inverse, lower, right)


def near_kernel(bits_ref, outer_ref, own_ref, partner_ref, sibling_ref, out_ref):
    low, high = bits_ref[0], bits_ref[1]
    quarter = own_ref.shape[0]
    half = 2 * quarter

    def columns(pair, side):
        return pl.ds(pl.multiple_of(pair * half + side * quarter, quarter), quarter)

    own = own_ref[...]
    for side, ref in ((low, own_ref), (1 - low, partner_ref)):
        base = outer_ref[:, columns(0, side)].astype(jnp.float32)
        out_ref[:, columns(high, side)] = (base - dot_turned(own, ref[...])).astype(jnp.bfloat16)
    out_ref[:, columns(1 - high, low)] = (-dot_turned(own, sibling_ref[...])).astype(jnp.bfloat16)


def far_kernel(place_ref, own_ref, far_ref, near_ref, out_ref):
    del place_ref, near_ref
    out_ref[...] = (-dot_turned(own_ref[...], far_ref[...])).astype(jnp.bfloat16)


def merged_near(bits, outer, own, partner, sibling):
    quarter = own.shape[0]
    return pl.pallas_call(
        near_kernel,
        out_shape=jax.ShapeDtypeStruct((quarter, 4 * quarter), jnp.bfloat16),
        in_specs=[pl.BlockSpec(memory_space=pltpu.SMEM), *in_vmem(4)],
        out_specs=pl.BlockSpec(memory_space=pltpu.VMEM),
        compiler_params=params(16),
        cost_estimate=estimate(5),
        name="merged_near",
    )(bits, outer, own, partner, sibling)


def merged_far(place, own, far, near):
    quarter, size = own.shape
    return pl.pallas_call(
        far_kernel,
        grid_spec=pltpu.PrefetchScalarGridSpec(
            num_scalar_prefetch=1,
            grid=(1,),
            in_specs=[
                pl.BlockSpec((quarter, size), lambda g, place: (0, 0)),
                pl.BlockSpec((quarter, size), lambda g, place: (0, 0)),
                pl.BlockSpec(memory_space=pl.ANY),
            ],
            out_specs=pl.BlockSpec((quarter, quarter), lambda g, place: (0, place[0])),
        ),
        out_shape=jax.ShapeDtypeStruct(near.shape, near.dtype),
        input_output_aliases={3: 0},
        compiler_params=params(16),
        cost_estimate=estimate(3),
        name="merged_far",
    )(place, own, far, near)


def laplacian(padded_ref, start, rows):
    above = padded_ref[start + 7 : start + 7 + rows, :]
    middle = padded_ref[start + 8 : start + 8 + rows, :]
    below = padded_ref[start + 9 : start + 9 + rows, :]
    column = lax.broadcasted_iota(jnp.int32, middle.shape, 1)
    last = middle.shape[1] - 1

    def sides(x):
        left = jnp.where(column == 0, 0.0, pltpu.roll(x, 1, 1))
        right = jnp.where(column == last, 0.0, pltpu.roll(x, last, 1))
        return left + right

    vertical = above + below
    edges = vertical + sides(middle)
    return (4.0 * edges + sides(vertical) - 20.0 * middle) / 6.0, middle


def gradient_kernel(
    wave_ref,
    medium_ref,
    source_ref,
    state_ref,
    adjoint_ref,
    above_ref,
    below_ref,
    receivers_ref,
    recorded_ref,
    out_ref,
    state_v,
    adjoint_v,
    placed_v,
):
    rows, columns = medium_ref.shape
    count = receivers_ref.shape[1]
    for n, (field_ref, padded) in enumerate(((state_ref, state_v), (adjoint_ref, adjoint_v))):
        padded[8 : 8 + rows, :] = field_ref[0].astype(jnp.float32)
        padded[7:8, :] = above_ref[n : n + 1, :]
        padded[8 + rows : 9 + rows, :] = below_ref[n : n + 1, :]
    cell = receivers_ref[...]
    cell_row = jnp.right_shift(cell, columns.bit_length() - 1)
    cell_column = jnp.bitwise_and(cell, columns - 1)
    row_hit = lax.broadcasted_iota(jnp.int32, (rows, count), 0) == cell_row
    column_hit = lax.broadcasted_iota(jnp.int32, (columns, count), 0) == cell_column
    column_one = jnp.where(column_hit, 1.0, 0.0).astype(jnp.bfloat16)
    at_column = dot(state_ref[0], column_one)
    value = jnp.sum(jnp.where(row_hit, at_column, 0.0), axis=0, keepdims=True)
    misfit = value - recorded_ref[...].astype(jnp.float32)
    parts = [
        jnp.where(row_hit, part.astype(jnp.float32), 0.0).astype(jnp.bfloat16)
        for part in split_three(misfit)
    ]
    placed_v[...] = dot_turned(
        jnp.concatenate(parts, axis=1), jnp.concatenate([column_one] * 3, axis=1)
    )
    kappa = 0.2 * (1.0 + wave_ref[0].astype(jnp.float32))
    kappa_sq = kappa * kappa
    step = 64
    for start in range(0, rows, step):
        r = slice(start, start + step)
        scaled = kappa_sq * medium_ref[r, :].astype(jnp.float32)
        smooth, state = laplacian(state_v, start, step)
        state_residual = source_ref[0, r, :].astype(jnp.float32) - (smooth + scaled * state)
        smooth, adjoint = laplacian(adjoint_v, start, step)
        adjoint_residual = placed_v[r, :] - (smooth + scaled * adjoint)
        out_ref[r, :] = -(kappa_sq * (state * state_residual + adjoint * adjoint_residual))


def edge_rows(state_field, adjoint_field):
    rows = state_field.shape[1]
    count = lax.axis_size("tile")
    forward = [(i, i + 1) for i in range(count - 1)]
    backward = [(target, source) for source, target in forward]
    last = jnp.concatenate([state_field[0, rows - 1 :], adjoint_field[0, rows - 1 :]], axis=0)
    first = jnp.concatenate([state_field[0, :1], adjoint_field[0, :1]], axis=0)
    above = lax.ppermute(last, "tile", forward).astype(jnp.float32)
    below = lax.ppermute(first, "tile", backward).astype(jnp.float32)
    return above, below


def gradient(
    wave_index, medium, source, state_field, adjoint_field, above, below, receivers, recorded
):
    rows, columns = medium.shape
    return pl.pallas_call(
        gradient_kernel,
        out_shape=jax.ShapeDtypeStruct((rows, columns), jnp.float32),
        in_specs=[pl.BlockSpec(memory_space=pltpu.SMEM), *in_vmem(8)],
        out_specs=pl.BlockSpec(memory_space=pltpu.VMEM),
        scratch_shapes=[
            pltpu.VMEM((rows + 16, columns), jnp.float32),
            pltpu.VMEM((rows + 16, columns), jnp.float32),
            pltpu.VMEM((rows, columns), jnp.float32),
        ],
        compiler_params=params(16),
        cost_estimate=estimate(5),
        name="gradient_term",
    )(
        wave_index, medium, source, state_field, adjoint_field, above, below, receivers, recorded
    )


def sum_over_near(term, near, far):
    index = lax.axis_index("freq")
    count = near * far
    share = term.shape[0] // count
    pieces = term.reshape(far, near, share, term.shape[1])
    mine = jnp.bitwise_and(index, near - 1)

    def piece(place):
        return lax.dynamic_index_in_dim(pieces, place, 1, keepdims=False)

    received = [piece(mine)]
    for shift in range(1, near):
        route = [
            (i, i // near * near + (i + shift) % near) for i in range(count)
        ]
        received.append(
            lax.ppermute(piece(jnp.bitwise_and(mine + shift, near - 1)), "freq", route)
        )
    return received


def sum_over_far(partial, near):
    index = lax.axis_index("freq")
    side = index // near
    route = [(i, (i + near) % (2 * near)) for i in range(2 * near)]
    kept = lax.dynamic_index_in_dim(partial, side, 0, keepdims=False)
    sent = lax.dynamic_index_in_dim(partial, 1 - side, 0, keepdims=False)
    return kept, lax.ppermute(sent, "freq", route)


def body(leaf_maps, wave_index, medium, source, state_field, adjoint_field, receivers, recorded):
    tie = lax.optimization_barrier
    tile_index = lax.axis_index("tile")
    low_bit = jnp.bitwise_and(tile_index, 1)
    high_bit = jnp.bitwise_and(jnp.right_shift(tile_index, 1), 1)
    low = low_bit[None]
    bits = jnp.stack([low_bit, high_bit])
    place = (2 * (1 - high_bit) + 1 - low_bit)[None]
    half = leaf_maps.shape[1] // 2
    near = lax.axis_size("freq") // 2

    partner_inner = from_partner(leaf_maps[0, half:, half:], "tile", 0)
    above, below = edge_rows(state_field, adjoint_field)
    term = gradient(
        wave_index, medium, source, state_field, adjoint_field, above, below, receivers, recorded
    )
    columns = leaf_maps[:, :half, : half // 2]
    partner_inner, term, columns = tie((partner_inner, term, columns))
    received = sum_over_near(term, near, 2)
    solved, own_triangle = first_solve(leaf_maps, partner_inner)
    solved, own_triangle, *received = tie((solved, own_triangle, *received))
    partner = from_partner(solved, "tile", 0)
    sibling_triangle = from_partner(own_triangle, "tile", 1)
    partner_triangle = from_partner(own_triangle, "tile", 0)
    kept, other = sum_over_far(functools.reduce(jnp.add, received), near)
    partner, kept = tie((partner, kept))
    cross, cross_part = cross_interface(low, solved, partner)
    sibling_triangle, cross_part = tie((sibling_triangle, cross_part))
    sibling_part = from_partner(cross_part, "tile", 1)
    far_triangle = from_partner(sibling_triangle, "tile", 0)
    outer, right = outer_blocks(low, columns, solved, partner)
    sibling_part, outer, right, other = tie((sibling_part, outer, right, other))
    gradient_rows = kept + other
    far_part = from_partner(sibling_part, "tile", 0)
    sibling_right = from_partner(right, "tile", 1)
    solved, inverse, lower = second_solve(
        low,
        (own_triangle, partner_triangle, sibling_triangle, far_triangle),
        cross,
        (sibling_part, far_part),
        right,
    )
    partner = from_partner(solved, "tile", 0)
    sibling = substitution(inverse, lower, sibling_right)
    sibling, partner = tie((sibling, partner))
    far = from_partner(sibling, "tile", 0)
    rows = merged_near(bits, outer, solved, partner, sibling)
    far, rows = tie((far, rows))
    rows = merged_far(place, solved, far, rows)
    return (rows[None], gradient_rows)


def solution(mesh):
    placed = (
        P("freq", "tile", None),
        P("freq"),
        P("tile", None),
        P("freq", "tile", None),
        P("freq", "tile", None),
        P("freq", "tile", None),
        P("freq", "tile"),
        P("freq", "tile"),
    )
    return jax.shard_map(
        body,
        mesh=mesh,
        in_specs=placed,
        out_specs=(P("freq", "tile", None), P(("tile", "freq"), None)),
        check_vma=False,
    )
```
